32 devices in a mesh: bond: 4 (over x, core), op: 8 (over z, y).
Axes of the slice: x: 2, y: 2, z: 4, core: 2. Of those that a mesh axis runs over, the one named last changes fastest.
Arguments:
- wave_slab: bfloat16 [8192, 8192], P('op', 'bond'), may hold values from -6 to 6
- left_blocks: bfloat16 [16, 16, 2, 128, 128], P('op'), may hold values from -0.375 to 0.375
- right_blocks: bfloat16 [16, 64, 2, 128, 128], P('op'), may hold values from -0.09375 to 0.09375
- sector_size: int32 [64], replicated, may hold values from 1 to 128
- left_pairs: int32 [16, 16, 2], P('op'), may hold values from 0 to 63
- right_pairs: int32 [16, 64, 2], P('op'), may hold values from 0 to 63
Outputs:
- applied: float32 [2048, 8192], P('bond', 'op')
The draws below stay inside these ranges and needn't reach their ends.
All inputs are finite; a program needn't handle non-finite values.
Results may differ from the reference program's by a relative error of at most 0.0029.
Values may be sent and summed in bfloat16 or wider, within the bound.
A program may use at most 128 MiB of HBM per device.

```python
import jax
import jax.numpy as jnp
from jax import lax

D = 8192
TILE = 128
NP = 2
RSEC = 16
K = 16
NSEC = 64
RROWS = 2048


def touch_ends(result, key, smallest, largest):
    place = [jax.random.randint(jax.random.fold_in(key, axis), (), 0, length) for axis, length in enumerate(result.shape)]
    main_axis = result.shape.index(max(result.shape))
    neighbour = place[:main_axis] + [(place[main_axis] + 1) % result.shape[main_axis]] + place[main_axis + 1:]
    return result.at[tuple(place)].set(smallest).at[tuple(neighbour)].set(largest)


def levels(key, dims, shards, smallest, high):
    loudness = 1.0
    for position, parts in shards:
        steps = jax.random.uniform(jax.random.fold_in(jax.random.fold_in(key, 6), position), (parts,), jnp.float32, smallest / len(shards), high / len(shards))
        loudness = loudness * jnp.repeat(jnp.exp(steps), dims[position] // parts).reshape((-1,) + (1,) * (len(dims) - 1 - position))
    return loudness


def gaussian(stream_key, extent, width, bound, cuts=(), kind=jnp.bfloat16):
    drawn = jax.random.normal(stream_key, extent, jnp.float32) * width
    if len(cuts) > 0:
        drawn = levels(stream_key, extent, cuts, -0.22, 0.18) * drawn
    return jnp.clip(drawn, min=-bound, max=bound).astype(kind)


def setup_inputs(seed: int = 0) -> dict:
    arg_keys = jax.random.split(jax.random.key(seed), 7)
    wave_slab = gaussian(arg_keys[0], (D, D), 1.0, 6.0, ((0, 8), (1, 4)))
    left_blocks = gaussian(arg_keys[1], (K, RSEC, NP, TILE, TILE), (NP * TILE) ** -0.5, 0.375, ((0, 8),))
    right_blocks = gaussian(arg_keys[2], (K, NSEC, NP, TILE, TILE), (NP * TILE * K) ** -0.5, 0.09375, ((0, 8),))
    sector_size = touch_ends(jax.random.randint(arg_keys[3], (NSEC,), 1, TILE + 1), jax.random.fold_in(arg_keys[3], 1), 1, TILE).astype(jnp.int32)
    left_pairs = touch_ends(jax.random.randint(arg_keys[4], (K, RSEC, NP), 0, NSEC), jax.random.fold_in(arg_keys[4], 1), 0, NSEC - 1).astype(jnp.int32)
    right_pairs = touch_ends(jax.random.randint(arg_keys[5], (K, NSEC, NP), 0, NSEC), jax.random.fold_in(arg_keys[5], 1), 0, NSEC - 1).astype(jnp.int32)
    return {"wave_slab": wave_slab, "left_blocks": left_blocks, "right_blocks": right_blocks, "sector_size": sector_size, "left_pairs": left_pairs, "right_pairs": right_pairs}


def live_mask(sector_size):
    states = jnp.arange(TILE, dtype=jnp.int32)
    return (states[None, :] < sector_size[:, None]).astype(jnp.float32).reshape(-1)


def reference(wave_slab, left_blocks, right_blocks, sector_size, left_pairs, right_pairs):
    live = live_mask(sector_size)
    masked = (wave_slab.astype(jnp.float32) * live[:, None] * live[None, :]).astype(jnp.bfloat16)
    sectors = masked.reshape(NSEC, TILE, D)

    def one_term(total, inputs):
        left_term, right_term, left_sel, right_sel = inputs
        picked = sectors[left_sel]
        middle = jnp.einsum("ipxy,ipyb->ixb", left_term.astype(jnp.float32), picked.astype(jnp.float32))
        middle = middle.astype(jnp.bfloat16).reshape(RROWS, NSEC, TILE)
        chosen = middle[:, right_sel]
        product = jnp.einsum("rjpy,jpyz->rjz", chosen.astype(jnp.float32), right_term.astype(jnp.float32))
        return total + product.reshape(RROWS, D), None

    start = jnp.zeros((RROWS, D), jnp.float32)
    total, _ = lax.scan(one_term, start, (left_blocks, right_blocks, left_pairs, right_pairs))
    return total * live[:RROWS, None] * live[None, :]
```

```python
import functools

import jax
import jax.numpy as jnp
from jax import lax
from jax.experimental import pallas as pl
from jax.experimental.pallas import tpu as pltpu
from jax.sharding import PartitionSpec as P

TILE = 128
PAIR = 2
PIECES = 2
VMEM = 48 * 1024 * 1024
MESH = pl.DeviceIdType.MESH
ANY = pl.BlockSpec(memory_space=pl.ANY)


def live_mask(sector_size):
    states = jnp.arange(TILE, dtype=jnp.int32)
    return (states[None, :] < sector_size[:, None]).astype(jnp.float32).reshape(-1)


def gather_kernel(line, wave, left, pairs, whole, lefts, pairs_out, loc_sem, swap_send, swap_recv, line_send, line_recv):
    op = lax.axis_index("op")
    z = op // PAIR
    y = op % PAIR
    partner = z * PAIR + (1 - y)
    rows = wave.shape[0]
    half = wave.shape[1] // PAIR
    cut = rows // PIECES
    barrier = pltpu.get_barrier_semaphore()

    def greet(other):
        pl.semaphore_signal(barrier, inc=1, device_id={"op": other}, device_id_type=MESH)

    greet(partner)

    @pl.when(z > 0)
    def _():
        greet(op - PAIR)

    @pl.when(z < line - 1)
    def _():
        greet(op + PAIR)

    neighbours = 1 + jnp.where(z > 0, 1, 0) + jnp.where(z < line - 1, 1, 0)
    pl.semaphore_wait(barrier, neighbours)

    def remote(src, dst, send, recv, other):
        return pltpu.make_async_remote_copy(
            src_ref=src, dst_ref=dst, send_sem=send, recv_sem=recv, device_id={"op": other}, device_id_type=MESH
        )

    def span(q):
        return pl.ds(q * cut, cut)

    swaps = []
    for q in range(PIECES):
        swaps.append(
            remote(
                wave.at[span(q), pl.ds(pl.multiple_of((1 - y) * half, TILE), half)],
                whole.at[z, y, span(q)],
                swap_send.at[q],
                swap_recv.at[q],
                partner,
            )
        )
    swaps.append(remote(left, lefts.at[y], swap_send.at[PIECES], swap_recv.at[PIECES], partner))
    swaps.append(remote(pairs, pairs_out.at[y], swap_send.at[PIECES + 1], swap_recv.at[PIECES + 1], partner))
    mine = wave.at[:, pl.ds(pl.multiple_of(y * half, TILE), half)]
    locals_ = [
        pltpu.make_async_copy(mine, whole.at[z, y], loc_sem.at[0]),
        pltpu.make_async_copy(left, lefts.at[y], loc_sem.at[1]),
        pltpu.make_async_copy(pairs, pairs_out.at[y], loc_sem.at[2]),
    ]

    def hop(way, step, mate, q):
        source = z - step if way == 0 else z + step
        owner = 1 - y if mate else y
        if step == 0 and not mate:
            src = wave.at[span(q), pl.ds(pl.multiple_of(y * half, TILE), half)]
        else:
            src = whole.at[source, owner, span(q)]
        other = op + PAIR if way == 0 else op - PAIR
        return remote(
            src,
            whole.at[source, owner, span(q)],
            line_send.at[way, step, mate, q],
            line_recv.at[way, step, mate, q],
            other,
        )

    places = (z, line - 1 - z)
    for c in swaps[:PIECES]:
        c.start()
    for step in range(line):
        for mate in range(PAIR):
            for q in range(PIECES):
                if step == 0 and mate:
                    swaps[q].wait_recv()
                for way in range(2):
                    if step > 0:

                        @pl.when(places[way] >= step)
                        def _():
                            hop(way, step - 1, mate, q).wait_recv()

                    if step < line - 1:

                        @pl.when((places[way] >= step) & (places[way] < line - 1))
                        def _():
                            hop(way, step, mate, q).start()

            if step == 0 and not mate:
                for c in swaps[PIECES:] + locals_:
                    c.start()
    for step in range(line - 1):
        for mate in range(PAIR):
            for q in range(PIECES):
                for way in range(2):

                    @pl.when((places[way] >= step) & (places[way] < line - 1))
                    def _():
                        hop(way, step, mate, q).wait_send()

    for c in swaps:
        c.wait_send()
    for c in swaps[PIECES:]:
        c.wait_recv()
    for c in locals_:
        c.wait()


def gather(wave, left, pairs, op_count):
    line = op_count // PAIR
    rows, strip = wave.shape
    hops = (2, max(line - 1, 1), PAIR, PIECES)
    return pl.pallas_call(
        functools.partial(gather_kernel, line),
        out_shape=(
            jax.ShapeDtypeStruct((line, PAIR, rows, strip // PAIR), wave.dtype),
            jax.ShapeDtypeStruct((PAIR,) + left.shape, left.dtype),
            jax.ShapeDtypeStruct((PAIR,) + pairs.shape, pairs.dtype),
        ),
        in_specs=[ANY] * 3,
        out_specs=(ANY,) * 3,
        scratch_shapes=[
            pltpu.SemaphoreType.DMA((3,)),
            pltpu.SemaphoreType.DMA((PIECES + 2,)),
            pltpu.SemaphoreType.DMA((PIECES + 2,)),
            pltpu.SemaphoreType.DMA(hops),
            pltpu.SemaphoreType.DMA(hops),
        ],
        compiler_params=pltpu.CompilerParams(collective_id=0, has_side_effects=True),
        name="gather",
    )(wave, left, pairs)


def exchange_kernel(count, place, target, x, out, loc_sem, send_sem, recv_sem):
    me = place()
    barrier = pltpu.get_barrier_semaphore()
    for d in range(1, count):
        pl.semaphore_signal(barrier, inc=1, device_id=target(lax.rem(me + d, count)), device_id_type=MESH)
    pl.semaphore_wait(barrier, count - 1)
    copies = []
    for d in range(1, count):
        to = lax.rem(me + d, count)
        copies.append(
            pltpu.make_async_remote_copy(
                src_ref=x.at[to],
                dst_ref=out.at[me],
                send_sem=send_sem.at[d],
                recv_sem=recv_sem.at[d],
                device_id=target(to),
                device_id_type=MESH,
            )
        )
    for c in copies:
        c.start()
    own = pltpu.make_async_copy(x.at[me], out.at[me], loc_sem)
    own.start()
    own.wait()
    for c in copies:
        c.wait()


def exchange(x, place, target, cid, name):
    count = x.shape[0]
    return pl.pallas_call(
        functools.partial(exchange_kernel, count, place, target),
        out_shape=jax.ShapeDtypeStruct(x.shape, x.dtype),
        in_specs=[ANY],
        out_specs=ANY,
        scratch_shapes=[
            pltpu.SemaphoreType.DMA,
            pltpu.SemaphoreType.DMA((count,)),
            pltpu.SemaphoreType.DMA((count,)),
        ],
        compiler_params=pltpu.CompilerParams(collective_id=cid, has_side_effects=True),
        name=name,
    )(x)


def plane_place():
    return lax.axis_index("bond") * PAIR + lax.axis_index("op") % PAIR


def plane_target(t):
    return {"bond": t // PAIR, "op": lax.axis_index("op") // PAIR * PAIR + t % PAIR}


def op_place():
    return lax.axis_index("op")


def op_target(t):
    return {"op": t}


def left_kernel(pairs, sizes, blocks, first, second, live, out):
    k, i = pl.program_id(0), pl.program_id(1)
    lane = lax.broadcasted_iota(jnp.int32, (TILE, TILE), 1)
    parts = []
    for p in range(2):
        block = blocks[0, 0, p].astype(jnp.float32)
        parts.append(jnp.where(lane < sizes[pairs[k, i, p]], block, 0.0).astype(jnp.bfloat16))
    a = jnp.concatenate(parts, axis=1)
    b = jnp.concatenate([first[0], second[0]], axis=0)
    out[0, 0] = (jnp.dot(a, b, preferred_element_type=jnp.float32) * live[...]).astype(out.dtype)


def left_product(sectors, lefts, pairs, sizes, live, bond_count):
    mates, terms, outs = lefts.shape[:3]
    half = sectors.shape[2]
    share = outs // bond_count
    blocks = lefts.reshape((mates * terms,) + lefts.shape[2:])
    return pl.pallas_call(
        left_kernel,
        out_shape=jax.ShapeDtypeStruct((bond_count * mates, terms, share * TILE, half), jnp.bfloat16),
        grid_spec=pltpu.PrefetchScalarGridSpec(
            num_scalar_prefetch=2,
            grid=(mates * terms, outs),
            in_specs=[
                pl.BlockSpec((1, 1, 2, TILE, TILE), lambda k, i, pr, sz: (k, i, 0, 0, 0)),
                pl.BlockSpec((1, TILE, half), lambda k, i, pr, sz: (pr[k, i, 0], 0, 0)),
                pl.BlockSpec((1, TILE, half), lambda k, i, pr, sz: (pr[k, i, 1], 0, 0)),
                pl.BlockSpec((1, half), lambda k, i, pr, sz: (0, 0)),
            ],
            out_specs=pl.BlockSpec(
                (1, 1, TILE, half),
                lambda k, i, pr, sz: (i // share * mates + k // terms, k % terms, i % share, 0),
            ),
        ),
        compiler_params=pltpu.CompilerParams(vmem_limit_bytes=VMEM),
        name="left_product",
    )(pairs, sizes, blocks, sectors, sectors, live)


def right_kernel(terms, pairs, blocks, *refs):
    out = refs[-1]
    a = jnp.concatenate([r[0, 0] for r in refs[:-1]], axis=1)
    b = blocks[:, 0].reshape(terms * 2 * TILE, TILE)
    out[0] = jnp.dot(a, b, preferred_element_type=jnp.float32).astype(out.dtype)


def right_product(arrived, right_blocks, pairs, op_count):
    _, terms, share_rows, half = arrived.shape
    sector_count = right_blocks.shape[1]
    per_src = half // TILE
    per_out = sector_count // op_count

    def picked(k, p):
        return pl.BlockSpec(
            (1, 1, share_rows, TILE), lambda j, pr: (pr[k, j, p] // per_src, k, 0, pr[k, j, p] % per_src)
        )

    specs = [picked(k, p) for k in range(terms) for p in range(2)]
    return pl.pallas_call(
        functools.partial(right_kernel, terms),
        out_shape=jax.ShapeDtypeStruct((op_count, share_rows, per_out * TILE), jnp.bfloat16),
        grid_spec=pltpu.PrefetchScalarGridSpec(
            num_scalar_prefetch=1,
            grid=(sector_count,),
            in_specs=[pl.BlockSpec((terms, 1, 2, TILE, TILE), lambda j, pr: (0, j, 0, 0, 0))] + specs,
            out_specs=pl.BlockSpec((1, share_rows, TILE), lambda j, pr: (j // per_out, 0, j % per_out)),
        ),
        compiler_params=pltpu.CompilerParams(vmem_limit_bytes=VMEM),
        name="right_product",
    )(pairs, right_blocks, *([arrived] * len(specs)))


def on_device(wave_slab, left_blocks, right_blocks, sector_size, left_pairs, right_pairs):
    live = live_mask(sector_size)
    op_count = lax.axis_size("op")
    bond_count = lax.axis_size("bond")
    op, bond = lax.axis_index("op"), lax.axis_index("bond")
    strip = wave_slab.shape[1]
    half = strip // PAIR
    flat = left_pairs.reshape(-1)
    padded = -(-flat.size // 1024) * 1024
    sent = jnp.pad(flat, (0, padded - flat.size)).reshape(-1, TILE)
    whole, lefts, both = gather(wave_slab, left_blocks, sent, op_count)
    pairs = both.reshape(PAIR, padded)[:, : flat.size].reshape((-1,) + left_pairs.shape[1:])
    half_live = lax.dynamic_slice_in_dim(live, bond * strip + op % PAIR * half, half)
    middle = left_product(whole.reshape(-1, TILE, half), lefts, pairs, sector_size, half_live[None, :], bond_count)
    arrived = exchange(middle, plane_place, plane_target, 1, "exchange_middle")
    partial = right_product(arrived, right_blocks, right_pairs, op_count)
    got = exchange(partial, op_place, op_target, 2, "exchange_sums")
    summed = jnp.sum(got.astype(jnp.float32), axis=0)
    share_rows, out_cols = summed.shape
    row_live = lax.dynamic_slice_in_dim(live, bond * share_rows, share_rows)
    col_live = lax.dynamic_slice_in_dim(live, op * out_cols, out_cols)
    return summed * row_live[:, None] * col_live[None, :]


def solution(mesh):
    placed = (
        P("op", "bond"),
        P("op", None, None, None, None),
        P("op", None, None, None, None),
        P(),
        P("op", None, None),
        P("op", None, None),
    )
    return jax.shard_map(
        on_device, mesh=mesh, in_specs=placed, out_specs=P("bond", "op"), check_vma=False
    )
```

```python
import functools

import jax
import jax.numpy as jnp
from jax import lax
from jax.experimental import pallas as pl
from jax.experimental.pallas import tpu as pltpu
from jax.sharding import PartitionSpec as P

TILE = 128
PAIR = 2
PIECES = 2
VMEM = 48 * 1024 * 1024
MESH = pl.DeviceIdType.MESH
ANY = pl.BlockSpec(memory_space=pl.ANY)


def live_mask(sector_size):
    states = jnp.arange(TILE, dtype=jnp.int32)
    return (states[None, :] < sector_size[:, None]).astype(jnp.float32).reshape(-1)


def gather_kernel(
    line, wave, left, right, pairs, whole, lefts, rights, pairs_out, loc_sem, swap_send, swap_recv, line_send, line_recv
):
    op = lax.axis_index("op")
    z = op // PAIR
    y = op % PAIR
    partner = z * PAIR + (1 - y)
    rows = wave.shape[0]
    half = wave.shape[1] // PAIR
    cut = rows // PIECES
    barrier = pltpu.get_barrier_semaphore()

    def greet(other):
        pl.semaphore_signal(barrier, inc=1, device_id={"op": other}, device_id_type=MESH)

    greet(partner)

    @pl.when(z > 0)
    def _():
        greet(op - PAIR)

    @pl.when(z < line - 1)
    def _():
        greet(op + PAIR)

    neighbours = 1 + jnp.where(z > 0, 1, 0) + jnp.where(z < line - 1, 1, 0)
    pl.semaphore_wait(barrier, neighbours)

    def remote(src, dst, send, recv, other):
        return pltpu.make_async_remote_copy(
            src_ref=src, dst_ref=dst, send_sem=send, recv_sem=recv, device_id={"op": other}, device_id_type=MESH
        )

    def span(q):
        return pl.ds(q * cut, cut)

    swaps = []
    for q in range(PIECES):
        swaps.append(
            remote(
                wave.at[span(q), pl.ds(pl.multiple_of((1 - y) * half, TILE), half)],
                whole.at[z, y, span(q)],
                swap_send.at[q],
                swap_recv.at[q],
                partner,
            )
        )
    swaps.append(remote(left, lefts.at[y], swap_send.at[PIECES], swap_recv.at[PIECES], partner))
    swaps.append(remote(pairs, pairs_out.at[y], swap_send.at[PIECES + 1], swap_recv.at[PIECES + 1], partner))
    swaps.append(remote(right, rights.at[y], swap_send.at[PIECES + 2], swap_recv.at[PIECES + 2], partner))
    mine = wave.at[:, pl.ds(pl.multiple_of(y * half, TILE), half)]
    locals_ = [
        pltpu.make_async_copy(mine, whole.at[z, y], loc_sem.at[0]),
        pltpu.make_async_copy(left, lefts.at[y], loc_sem.at[1]),
        pltpu.make_async_copy(pairs, pairs_out.at[y], loc_sem.at[2]),
        pltpu.make_async_copy(right, rights.at[y], loc_sem.at[3]),
    ]

    def hop(way, step, mate, q):
        source = z - step if way == 0 else z + step
        owner = 1 - y if mate else y
        if step == 0 and not mate:
            src = wave.at[span(q), pl.ds(pl.multiple_of(y * half, TILE), half)]
        else:
            src = whole.at[source, owner, span(q)]
        other = op + PAIR if way == 0 else op - PAIR
        return remote(
            src,
            whole.at[source, owner, span(q)],
            line_send.at[way, step, mate, q],
            line_recv.at[way, step, mate, q],
            other,
        )

    places = (z, line - 1 - z)
    for c in swaps[:PIECES]:
        c.start()
    for step in range(line):
        for mate in range(PAIR):
            for q in range(PIECES):
                if step == 0 and mate:
                    swaps[q].wait_recv()
                for way in range(2):
                    if step > 0:

                        @pl.when(places[way] >= step)
                        def _():
                            hop(way, step - 1, mate, q).wait_recv()

                    if step < line - 1:

                        @pl.when((places[way] >= step) & (places[way] < line - 1))
                        def _():
                            hop(way, step, mate, q).start()

            if step == 0 and not mate:
                for c in swaps[PIECES:] + locals_:
                    c.start()
    for step in range(line - 1):
        for mate in range(PAIR):
            for q in range(PIECES):
                for way in range(2):

                    @pl.when((places[way] >= step) & (places[way] < line - 1))
                    def _():
                        hop(way, step, mate, q).wait_send()

    for c in swaps:
        c.wait_send()
    for c in swaps[PIECES:]:
        c.wait_recv()
    for c in locals_:
        c.wait()


def gather(wave, left, right, pairs, op_count):
    line = op_count // PAIR
    rows, strip = wave.shape
    hops = (2, max(line - 1, 1), PAIR, PIECES)
    return pl.pallas_call(
        functools.partial(gather_kernel, line),
        out_shape=(
            jax.ShapeDtypeStruct((line, PAIR, rows, strip // PAIR), wave.dtype),
            jax.ShapeDtypeStruct((PAIR,) + left.shape, left.dtype),
            jax.ShapeDtypeStruct((PAIR,) + right.shape, right.dtype),
            jax.ShapeDtypeStruct((PAIR,) + pairs.shape, pairs.dtype),
        ),
        in_specs=[ANY] * 4,
        out_specs=(ANY,) * 4,
        scratch_shapes=[
            pltpu.SemaphoreType.DMA((4,)),
            pltpu.SemaphoreType.DMA((PIECES + 3,)),
            pltpu.SemaphoreType.DMA((PIECES + 3,)),
            pltpu.SemaphoreType.DMA(hops),
            pltpu.SemaphoreType.DMA(hops),
        ],
        compiler_params=pltpu.CompilerParams(collective_id=0, has_side_effects=True),
        name="gather",
    )(wave, left, right, pairs)


def exchange_kernel(count, place, target, x, out, loc_sem, send_sem, recv_sem):
    me = place()
    barrier = pltpu.get_barrier_semaphore()
    for d in range(1, count):
        pl.semaphore_signal(barrier, inc=1, device_id=target(lax.rem(me + d, count)), device_id_type=MESH)
    pl.semaphore_wait(barrier, count - 1)
    copies = []
    for d in range(1, count):
        to = lax.rem(me + d, count)
        copies.append(
            pltpu.make_async_remote_copy(
                src_ref=x.at[to],
                dst_ref=out.at[me],
                send_sem=send_sem.at[d],
                recv_sem=recv_sem.at[d],
                device_id=target(to),
                device_id_type=MESH,
            )
        )
    for c in copies:
        c.start()
    own = pltpu.make_async_copy(x.at[me], out.at[me], loc_sem)
    own.start()
    own.wait()
    for c in copies:
        c.wait()


def exchange(x, place, target, cid, name):
    count = x.shape[0]
    return pl.pallas_call(
        functools.partial(exchange_kernel, count, place, target),
        out_shape=jax.ShapeDtypeStruct(x.shape, x.dtype),
        in_specs=[ANY],
        out_specs=ANY,
        scratch_shapes=[
            pltpu.SemaphoreType.DMA,
            pltpu.SemaphoreType.DMA((count,)),
            pltpu.SemaphoreType.DMA((count,)),
        ],
        compiler_params=pltpu.CompilerParams(collective_id=cid, has_side_effects=True),
        name=name,
    )(x)


def plane_place():
    return lax.axis_index("bond") * PAIR + lax.axis_index("op") % PAIR


def plane_target(t):
    return {"bond": t // PAIR, "op": lax.axis_index("op") // PAIR * PAIR + t % PAIR}


def op_place():
    return lax.axis_index("op")


def op_target(t):
    return {"op": t}


RESIDENT = dict(pipeline_mode=pl.Buffered(buffer_count=1))


def left_kernel(pairs, sizes, blocks, sectors, live, out):
    k, i = pl.program_id(0), pl.program_id(1)
    lane = lax.broadcasted_iota(jnp.int32, (TILE, TILE), 1)
    parts, picks = [], []
    for p in range(2):
        pick = pairs[k, i, p]
        block = blocks[0, 0, p].astype(jnp.float32)
        parts.append(jnp.where(lane < sizes[pick], block, 0.0).astype(jnp.bfloat16))
        picks.append(sectors[pick])
    a = jnp.concatenate(parts, axis=1)
    b = jnp.concatenate(picks, axis=0)
    out[0, 0] = (jnp.dot(a, b, preferred_element_type=jnp.float32) * live[...]).astype(out.dtype)


def left_product(sectors, lefts, pairs, sizes, live, plane):
    terms, outs = lefts.shape[:2]
    half = sectors.shape[2]
    share = outs // plane
    return pl.pallas_call(
        left_kernel,
        out_shape=jax.ShapeDtypeStruct((plane, terms, share * TILE, half), jnp.bfloat16),
        grid_spec=pltpu.PrefetchScalarGridSpec(
            num_scalar_prefetch=2,
            grid=(terms, outs),
            in_specs=[
                pl.BlockSpec((1, 1, 2, TILE, TILE), lambda k, i, pr, sz: (k, i, 0, 0, 0)),
                pl.BlockSpec(sectors.shape, lambda k, i, pr, sz: (0, 0, 0), **RESIDENT),
                pl.BlockSpec((1, half), lambda k, i, pr, sz: (0, 0)),
            ],
            out_specs=pl.BlockSpec((1, 1, TILE, half), lambda k, i, pr, sz: (i // share, k, i % share, 0)),
        ),
        compiler_params=pltpu.CompilerParams(vmem_limit_bytes=VMEM),
        name="left_product",
    )(pairs, sizes, lefts, sectors, live)


def right_kernel(terms, pairs, blocks, arrived, out):
    j = pl.program_id(0)
    per_src = arrived.shape[3] // TILE
    picks = []
    for k in range(terms):
        for p in range(2):
            s = pairs[k, j, p]
            lanes = pl.ds(pl.multiple_of(s % per_src * TILE, TILE), TILE)
            picks.append(arrived[s // per_src, k, :, lanes])
    a = jnp.concatenate(picks, axis=1)
    b = blocks[:, 0].reshape(terms * 2 * TILE, TILE)
    out[0] = jnp.dot(a, b, preferred_element_type=jnp.float32).astype(out.dtype)


def right_product(arrived, rights, pairs, op_count):
    _, terms, rows, _ = arrived.shape
    sector_count = rights.shape[1]
    per_out = sector_count // op_count
    return pl.pallas_call(
        functools.partial(right_kernel, terms),
        out_shape=jax.ShapeDtypeStruct((op_count, rows, per_out * TILE), jnp.bfloat16),
        grid_spec=pltpu.PrefetchScalarGridSpec(
            num_scalar_prefetch=1,
            grid=(sector_count,),
            in_specs=[
                pl.BlockSpec((terms, 1, 2, TILE, TILE), lambda j, pr: (0, j, 0, 0, 0)),
                pl.BlockSpec(arrived.shape, lambda j, pr: (0, 0, 0, 0), **RESIDENT),
            ],
            out_specs=pl.BlockSpec((1, rows, TILE), lambda j, pr: (j // per_out, 0, j % per_out)),
        ),
        compiler_params=pltpu.CompilerParams(vmem_limit_bytes=VMEM),
        name="right_product",
    )(pairs, rights, arrived)


def on_device(wave_slab, left_blocks, right_blocks, sector_size, left_pairs, right_pairs):
    live = live_mask(sector_size)
    op_count = lax.axis_size("op")
    bond_count = lax.axis_size("bond")
    op, bond = lax.axis_index("op"), lax.axis_index("bond")
    strip = wave_slab.shape[1]
    half = strip // PAIR
    flat = jnp.concatenate([left_pairs.reshape(-1), right_pairs.reshape(-1)])
    padded = -(-flat.size // 1024) * 1024
    sent = jnp.pad(flat, (0, padded - flat.size)).reshape(-1, TILE)
    whole, lefts, rights, both = gather(wave_slab, left_blocks, right_blocks, sent, op_count)
    both = both.reshape(PAIR, padded)
    lefts_at = both[:, : left_pairs.size].reshape((-1,) + left_pairs.shape[1:])
    rights_at = both[:, left_pairs.size : flat.size].reshape((-1,) + right_pairs.shape[1:])
    lefts = lefts.reshape((-1,) + left_blocks.shape[1:])
    rights = rights.reshape((-1,) + right_blocks.shape[1:])
    half_live = lax.dynamic_slice_in_dim(live, bond * strip + op % PAIR * half, half)
    sectors = whole.reshape(-1, TILE, half)
    middle = left_product(sectors, lefts, lefts_at, sector_size, half_live[None, :], bond_count * PAIR)
    arrived = exchange(middle, plane_place, plane_target, 1, "exchange_middle")
    partial = right_product(arrived, rights, rights_at, op_count)
    got = exchange(partial, op_place, op_target, 2, "exchange_sums")
    got = got.reshape((-1, PAIR) + got.shape[1:])
    summed = jnp.sum(got.astype(jnp.float32), axis=0).reshape(-1, got.shape[3])
    share_rows, out_cols = summed.shape
    row_live = lax.dynamic_slice_in_dim(live, bond * share_rows, share_rows)
    col_live = lax.dynamic_slice_in_dim(live, op * out_cols, out_cols)
    return summed * row_live[:, None] * col_live[None, :]


def solution(mesh):
    placed = (
        P("op", "bond"),
        P("op", None, None, None, None),
        P("op", None, None, None, None),
        P(),
        P("op", None, None),
        P("op", None, None),
    )
    return jax.shard_map(
        on_device, mesh=mesh, in_specs=placed, out_specs=P("bond", "op"), check_vma=False
    )
```

```python
import functools

import jax
import jax.numpy as jnp
from jax import lax
from jax.experimental import pallas as pl
from jax.experimental.pallas import tpu as pltpu
from jax.sharding import PartitionSpec as P

TILE = 128
PAIR = 2
PIECES = 2
SLICES = 8
VMEM = 48 * 1024 * 1024
MESH = pl.DeviceIdType.MESH
ANY = pl.BlockSpec(memory_space=pl.ANY)


def live_mask(sector_size):
    states = jnp.arange(TILE, dtype=jnp.int32)
    return (states[None, :] < sector_size[:, None]).astype(jnp.float32).reshape(-1)


def gather_kernel(
    line, wave, left, right, pairs, whole, lefts, rights, pairs_out, loc_sem, swap_send, swap_recv, line_send, line_recv
):
    op = lax.axis_index("op")
    z = op // PAIR
    y = op % PAIR
    partner = z * PAIR + (1 - y)
    rows = wave.shape[0]
    half = wave.shape[1] // PAIR
    cut = rows // PIECES
    barrier = pltpu.get_barrier_semaphore()

    def greet(other):
        pl.semaphore_signal(barrier, inc=1, device_id={"op": other}, device_id_type=MESH)

    greet(partner)

    @pl.when(z > 0)
    def _():
        greet(op - PAIR)

    @pl.when(z < line - 1)
    def _():
        greet(op + PAIR)

    neighbours = 1 + jnp.where(z > 0, 1, 0) + jnp.where(z < line - 1, 1, 0)
    pl.semaphore_wait(barrier, neighbours)

    def remote(src, dst, send, recv, other):
        return pltpu.make_async_remote_copy(
            src_ref=src, dst_ref=dst, send_sem=send, recv_sem=recv, device_id={"op": other}, device_id_type=MESH
        )

    def span(q):
        return pl.ds(q * cut, cut)

    swaps = []
    for q in range(PIECES):
        swaps.append(
            remote(
                wave.at[span(q), pl.ds(pl.multiple_of((1 - y) * half, TILE), half)],
                whole.at[z, y, span(q)],
                swap_send.at[q],
                swap_recv.at[q],
                partner,
            )
        )
    swaps.append(remote(left, lefts.at[y], swap_send.at[PIECES], swap_recv.at[PIECES], partner))
    swaps.append(remote(pairs, pairs_out.at[y], swap_send.at[PIECES + 1], swap_recv.at[PIECES + 1], partner))
    part = right.shape[1] // SLICES
    for n in range(SLICES):
        some = pl.ds(n * part, part)
        place = PIECES + 2 + n
        swaps.append(
            remote(right.at[:, some], rights.at[y, :, some], swap_send.at[place], swap_recv.at[place], partner)
        )
    mine = wave.at[:, pl.ds(pl.multiple_of(y * half, TILE), half)]
    locals_ = [
        pltpu.make_async_copy(mine, whole.at[z, y], loc_sem.at[0]),
        pltpu.make_async_copy(left, lefts.at[y], loc_sem.at[1]),
        pltpu.make_async_copy(pairs, pairs_out.at[y], loc_sem.at[2]),
        pltpu.make_async_copy(right, rights.at[y], loc_sem.at[3]),
    ]

    def hop(way, step, mate, q):
        source = z - step if way == 0 else z + step
        owner = 1 - y if mate else y
        if step == 0 and not mate:
            src = wave.at[span(q), pl.ds(pl.multiple_of(y * half, TILE), half)]
        else:
            src = whole.at[source, owner, span(q)]
        other = op + PAIR if way == 0 else op - PAIR
        return remote(
            src,
            whole.at[source, owner, span(q)],
            line_send.at[way, step, mate, q],
            line_recv.at[way, step, mate, q],
            other,
        )

    places = (z, line - 1 - z)
    for c in swaps[:PIECES]:
        c.start()
    waiting = swaps[PIECES + 2 :] + swaps[PIECES : PIECES + 2] + locals_
    for step in range(line):
        for mate in range(PAIR):
            for q in range(PIECES):
                if step == 0 and mate:
                    swaps[q].wait_recv()
                for way in range(2):
                    if step > 0:

                        @pl.when(places[way] >= step)
                        def _():
                            hop(way, step - 1, mate, q).wait_recv()

                    if step < line - 1:

                        @pl.when((places[way] >= step) & (places[way] < line - 1))
                        def _():
                            hop(way, step, mate, q).start()

                if waiting:
                    waiting.pop(0).start()

    for c in waiting:
        c.start()
    for step in range(line - 1):
        for mate in range(PAIR):
            for q in range(PIECES):
                for way in range(2):

                    @pl.when((places[way] >= step) & (places[way] < line - 1))
                    def _():
                        hop(way, step, mate, q).wait_send()

    for c in swaps:
        c.wait_send()
    for c in swaps[PIECES:]:
        c.wait_recv()
    for c in locals_:
        c.wait()


def gather(wave, left, right, pairs, op_count):
    line = op_count // PAIR
    rows, strip = wave.shape
    hops = (2, max(line - 1, 1), PAIR, PIECES)
    return pl.pallas_call(
        functools.partial(gather_kernel, line),
        out_shape=(
            jax.ShapeDtypeStruct((line, PAIR, rows, strip // PAIR), wave.dtype),
            jax.ShapeDtypeStruct((PAIR,) + left.shape, left.dtype),
            jax.ShapeDtypeStruct((PAIR,) + right.shape, right.dtype),
            jax.ShapeDtypeStruct((PAIR,) + pairs.shape, pairs.dtype),
        ),
        in_specs=[ANY] * 4,
        out_specs=(ANY,) * 4,
        scratch_shapes=[
            pltpu.SemaphoreType.DMA((4,)),
            pltpu.SemaphoreType.DMA((PIECES + 2 + SLICES,)),
            pltpu.SemaphoreType.DMA((PIECES + 2 + SLICES,)),
            pltpu.SemaphoreType.DMA(hops),
            pltpu.SemaphoreType.DMA(hops),
        ],
        compiler_params=pltpu.CompilerParams(collective_id=0, has_side_effects=True),
        name="gather",
    )(wave, left, right, pairs)


def exchange_kernel(count, place, target, x, out, loc_sem, send_sem, recv_sem):
    me = place()
    barrier = pltpu.get_barrier_semaphore()
    for d in range(1, count):
        pl.semaphore_signal(barrier, inc=1, device_id=target(lax.rem(me + d, count)), device_id_type=MESH)
    pl.semaphore_wait(barrier, count - 1)
    copies = []
    for d in range(1, count):
        to = lax.rem(me + d, count)
        copies.append(
            pltpu.make_async_remote_copy(
                src_ref=x.at[to],
                dst_ref=out.at[me],
                send_sem=send_sem.at[d],
                recv_sem=recv_sem.at[d],
                device_id=target(to),
                device_id_type=MESH,
            )
        )
    for c in copies:
        c.start()
    own = pltpu.make_async_copy(x.at[me], out.at[me], loc_sem)
    own.start()
    own.wait()
    for c in copies:
        c.wait()


def exchange(x, place, target, cid, name):
    count = x.shape[0]
    return pl.pallas_call(
        functools.partial(exchange_kernel, count, place, target),
        out_shape=jax.ShapeDtypeStruct(x.shape, x.dtype),
        in_specs=[ANY],
        out_specs=ANY,
        scratch_shapes=[
            pltpu.SemaphoreType.DMA,
            pltpu.SemaphoreType.DMA((count,)),
            pltpu.SemaphoreType.DMA((count,)),
        ],
        compiler_params=pltpu.CompilerParams(collective_id=cid, has_side_effects=True),
        name=name,
    )(x)


def plane_place():
    return lax.axis_index("bond") * PAIR + lax.axis_index("op") % PAIR


def plane_target(t):
    return {"bond": t // PAIR, "op": lax.axis_index("op") // PAIR * PAIR + t % PAIR}


def op_place():
    return lax.axis_index("op")


def op_target(t):
    return {"op": t}


RESIDENT = dict(pipeline_mode=pl.Buffered(buffer_count=1))


def left_kernel(pairs, sizes, blocks, sectors, live, out):
    k, i = pl.program_id(0), pl.program_id(1)
    lane = lax.broadcasted_iota(jnp.int32, (TILE, TILE), 1)
    parts, picks = [], []
    for p in range(2):
        pick = pairs[k, i, p]
        block = blocks[0, 0, p].astype(jnp.float32)
        parts.append(jnp.where(lane < sizes[pick], block, 0.0).astype(jnp.bfloat16))
        picks.append(sectors[pick])
    a = jnp.concatenate(parts, axis=1)
    b = jnp.concatenate(picks, axis=0)
    out[0, 0] = (jnp.dot(a, b, preferred_element_type=jnp.float32) * live[...]).astype(out.dtype)


def left_product(sectors, lefts, pairs, sizes, live, plane):
    terms, outs = lefts.shape[:2]
    half = sectors.shape[2]
    share = outs // plane
    return pl.pallas_call(
        left_kernel,
        out_shape=jax.ShapeDtypeStruct((plane, terms, share * TILE, half), jnp.bfloat16),
        grid_spec=pltpu.PrefetchScalarGridSpec(
            num_scalar_prefetch=2,
            grid=(terms, outs),
            in_specs=[
                pl.BlockSpec((1, 1, 2, TILE, TILE), lambda k, i, pr, sz: (k, i, 0, 0, 0)),
                pl.BlockSpec(sectors.shape, lambda k, i, pr, sz: (0, 0, 0), **RESIDENT),
                pl.BlockSpec((1, half), lambda k, i, pr, sz: (0, 0)),
            ],
            out_specs=pl.BlockSpec((1, 1, TILE, half), lambda k, i, pr, sz: (i // share, k, i % share, 0)),
        ),
        compiler_params=pltpu.CompilerParams(vmem_limit_bytes=VMEM),
        name="left_product",
    )(pairs, sizes, lefts, sectors, live)


def right_kernel(terms, pairs, blocks, arrived, out):
    j = pl.program_id(0)
    per_src = arrived.shape[3] // TILE
    picks = []
    for k in range(terms):
        for p in range(2):
            s = pairs[k, j, p]
            lanes = pl.ds(pl.multiple_of(s % per_src * TILE, TILE), TILE)
            picks.append(arrived[s // per_src, k, :, lanes])
    a = jnp.concatenate(picks, axis=1)
    b = blocks[:, 0].reshape(terms * 2 * TILE, TILE)
    out[0] = jnp.dot(a, b, preferred_element_type=jnp.float32).astype(out.dtype)


def right_product(arrived, rights, pairs, op_count):
    _, terms, rows, _ = arrived.shape
    sector_count = rights.shape[1]
    per_out = sector_count // op_count
    return pl.pallas_call(
        functools.partial(right_kernel, terms),
        out_shape=jax.ShapeDtypeStruct((op_count, rows, per_out * TILE), jnp.bfloat16),
        grid_spec=pltpu.PrefetchScalarGridSpec(
            num_scalar_prefetch=1,
            grid=(sector_count,),
            in_specs=[
                pl.BlockSpec((terms, 1, 2, TILE, TILE), lambda j, pr: (0, j, 0, 0, 0)),
                pl.BlockSpec(arrived.shape, lambda j, pr: (0, 0, 0, 0), **RESIDENT),
            ],
            out_specs=pl.BlockSpec((1, rows, TILE), lambda j, pr: (j // per_out, 0, j % per_out)),
        ),
        compiler_params=pltpu.CompilerParams(vmem_limit_bytes=VMEM),
        name="right_product",
    )(pairs, rights, arrived)


def on_device(wave_slab, left_blocks, right_blocks, sector_size, left_pairs, right_pairs):
    live = live_mask(sector_size)
    op_count = lax.axis_size("op")
    bond_count = lax.axis_size("bond")
    op, bond = lax.axis_index("op"), lax.axis_index("bond")
    strip = wave_slab.shape[1]
    half = strip // PAIR
    flat = jnp.concatenate([left_pairs.reshape(-1), right_pairs.reshape(-1)])
    padded = -(-flat.size // 1024) * 1024
    sent = jnp.pad(flat, (0, padded - flat.size)).reshape(-1, TILE)
    whole, lefts, rights, both = gather(wave_slab, left_blocks, right_blocks, sent, op_count)
    both = both.reshape(PAIR, padded)
    lefts_at = both[:, : left_pairs.size].reshape((-1,) + left_pairs.shape[1:])
    rights_at = both[:, left_pairs.size : flat.size].reshape((-1,) + right_pairs.shape[1:])
    lefts = lefts.reshape((-1,) + left_blocks.shape[1:])
    rights = rights.reshape((-1,) + right_blocks.shape[1:])
    half_live = lax.dynamic_slice_in_dim(live, bond * strip + op % PAIR * half, half)
    sectors = whole.reshape(-1, TILE, half)
    middle = left_product(sectors, lefts, lefts_at, sector_size, half_live[None, :], bond_count * PAIR)
    arrived = exchange(middle, plane_place, plane_target, 1, "exchange_middle")
    partial = right_product(arrived, rights, rights_at, op_count)
    got = exchange(partial, op_place, op_target, 2, "exchange_sums")
    got = got.reshape((-1, PAIR) + got.shape[1:])
    summed = jnp.sum(got.astype(jnp.float32), axis=0).reshape(-1, got.shape[3])
    share_rows, out_cols = summed.shape
    row_live = lax.dynamic_slice_in_dim(live, bond * share_rows, share_rows)
    col_live = lax.dynamic_slice_in_dim(live, op * out_cols, out_cols)
    return summed * row_live[:, None] * col_live[None, :]


def solution(mesh):
    placed = (
        P("op", "bond"),
        P("op", None, None, None, None),
        P("op", None, None, None, None),
        P(),
        P("op", None, None),
        P("op", None, None),
    )
    return jax.shard_map(
        on_device, mesh=mesh, in_specs=placed, out_specs=P("bond", "op"), check_vma=False
    )
```
